128 devices in a mesh: slide: 4 (over y), gy: 4 (over z), gx: 8 (over x, core).
Axes of the slice: x: 4, y: 4, z: 4, core: 2. Of those that a mesh axis runs over, the one named last changes fastest.
Arguments:
- feature_map: bfloat16 [2048, 1024, 256], P(('slide', 'gy'), 'gx'), parts along dimension 0, may hold values from -6 to 6
- depth_kernel: float32 [7, 7, 256], replicated, may hold values from -0.875 to 0.875
- depth_bias: float32 [256], replicated, may hold values from -3 to 3
- norm_gain: float32 [256], replicated, may hold values from 0.1 to 1.9
- norm_bias: float32 [256], replicated, may hold values from -3 to 3
- up_weight: bfloat16 [256, 1024], replicated, may hold values from -0.375 to 0.375
- up_bias: float32 [1024], replicated, may hold values from -3 to 3
- down_weight: bfloat16 [1024, 256], replicated, may hold values from -0.1875 to 0.1875
- down_bias: float32 [256], replicated, may hold values from -3 to 3
- layer_scale: float32 [256], replicated, may hold values from 0.5 to 1.5
- tile_route: int32 [128, 96], P(('slide', 'gy', 'gx')), parts along dimension 0, may hold values from -1 to 127, as said below
Outputs:
- balanced_tiles: bfloat16 [6144, 128, 256], P(('slide', 'gy', 'gx')), parts along dimension 0
The draws below stay inside these ranges and needn't reach their ends.
There are 4 independent parts, one for each index of `slide`. The reference program is written for one: setup_inputs(seed, part) draws one part's arguments, and reference() takes and returns one part's arrays. A program takes and returns all parts, laid end to end along the dimension named above; an argument that names none is the same for every part. Nothing has to cross between parts.
Inputs may be any that keep to these rules, and one draw needn't show every extreme that they name: `tile_route`: each entry is a tile index of the sending device or -1. Every device's listed tiles are distinct, one device lists exactly 96 tiles and none more, and the entries that are not -1 for one receiver number at most 48, exactly 48 for some receiver.
All inputs are finite; a program needn't handle non-finite values.
Results may differ from the reference program's by a relative error of at most 0.0049.
Values may be sent and summed in bfloat16 or wider, within the bound.
A program may use at most 192 MiB of HBM per device.

```python
import jax
import jax.numpy as jnp
from jax import lax

C = 256
HID = 1024
KS = 7
W_DEV = 128
H_DEV = 128
GRID_Y = 4
GRID_X = 8
DEV_GRID = 32
MOST = 96
RECV = 48
SLOT = 3
MAP_H = 512
MAP_W = 1024


def draw_tile_route(key, part):
    grid = DEV_GRID
    keys = jax.random.split(key, 4)
    spare = jax.random.randint(keys[0], (), 0, grid)
    total = RECV * grid - spare
    heavy = jax.random.randint(keys[1], (), 0, grid)
    device_ids = jnp.arange(grid, dtype=jnp.int32)
    weights = jax.random.randint(keys[2], (grid,), 2, 5)
    weights = jnp.where(device_ids == heavy, 0, weights)
    rest = total - MOST
    running = jnp.cumsum(weights)
    bounds = rest * running // running[-1]
    counts = bounds - jnp.concatenate([jnp.zeros((1,), jnp.int32), bounds[:-1]])
    counts = jnp.where(device_ids == heavy, MOST, counts).astype(jnp.int32)
    starts = (jnp.cumsum(counts) - counts).astype(jnp.int32)
    perm_keys = jax.random.split(keys[3], grid)
    orders = jax.vmap(lambda k: jax.random.permutation(k, H_DEV))(perm_keys).astype(jnp.int32)
    listed = jnp.arange(MOST, dtype=jnp.int32)
    target = (starts[:, None] + listed[None, :]) % grid
    column = target * SLOT + listed[None, :] // grid
    values = jnp.where(listed[None, :] < counts[:, None], orders[:, :MOST], -1)
    table = jnp.zeros((grid, grid * SLOT), jnp.int32)
    rows_idx = jnp.broadcast_to(device_ids[:, None], (grid, MOST))
    return table.at[rows_idx, column].set(values.astype(jnp.int32))


def level_of(stream_key, extent, cuts, smallest, top_value):
    loudness = 1.0
    for axis_at, shards_of in cuts:
        draws = jax.random.uniform(jax.random.fold_in(jax.random.fold_in(stream_key, 6), axis_at), (shards_of,), jnp.float32, smallest / len(cuts), top_value / len(cuts))
        loudness = loudness * jnp.repeat(jnp.exp(draws), extent[axis_at] // shards_of).reshape((-1,) + (1,) * (len(extent) - 1 - axis_at))
    return loudness


def noise(stream_key, extent, width, limit, pieces=(), kind=jnp.bfloat16):
    array = jax.random.normal(stream_key, extent, jnp.float32) * width
    if len(pieces) > 0:
        array = level_of(stream_key, extent, pieces, -0.22, 0.18) * array
    return jnp.clip(array, min=-limit, max=limit).astype(kind)


def setup_inputs(seed: int = 0, part: int = 0) -> dict:
    arg_keys = jax.random.split(jax.random.key(seed), 12)
    own_keys = jax.random.split(jax.random.fold_in(arg_keys[11], part), 12)
    feature_map = noise(own_keys[0], (MAP_H, MAP_W, C), 1.0, 6.0, ((0, 4), (1, 8)))
    depth_kernel = noise(arg_keys[1], (KS, KS, C), (KS * KS) ** -0.5, 0.875, (), jnp.float32)
    depth_bias = noise(arg_keys[2], (C,), 0.5, 3.0, (), jnp.float32)
    norm_gain = jnp.clip(1.0 + 0.18 * jax.random.normal(arg_keys[3], (C,), jnp.float32), 0.1, 1.9)
    norm_bias = noise(arg_keys[4], (C,), 0.5, 3.0, (), jnp.float32)
    up_weight = noise(arg_keys[5], (C, HID), C ** -0.5, 0.375)
    up_bias = noise(arg_keys[6], (HID,), 0.5, 3.0, (), jnp.float32)
    down_weight = noise(arg_keys[7], (HID, C), HID ** -0.5, 0.1875)
    down_bias = noise(arg_keys[8], (C,), 0.5, 3.0, (), jnp.float32)
    layer_scale = jnp.clip(jax.random.uniform(arg_keys[9], (C,), jnp.float32, 0.5, 1.5), 0.5, 1.5)
    tile_route = draw_tile_route(jax.random.fold_in(jax.random.fold_in(arg_keys[11], part), 71), part)
    return {"feature_map": feature_map, "depth_kernel": depth_kernel, "depth_bias": depth_bias, "norm_gain": norm_gain, "norm_bias": norm_bias, "up_weight": up_weight, "up_bias": up_bias, "down_weight": down_weight, "down_bias": down_bias, "layer_scale": layer_scale, "tile_route": tile_route}


def pointwise(x_tiles, dw_tiles, norm_gain, norm_bias, up_weight, up_bias, down_weight, down_bias, layer_scale):
    rows = dw_tiles.reshape(-1, dw_tiles.shape[-1]).astype(jnp.float32)
    center = lax.optimization_barrier(jnp.mean(rows, axis=1, keepdims=True))
    spread = lax.optimization_barrier(jnp.mean((rows - center) ** 2, axis=1, keepdims=True))
    normed = ((rows - center) / jnp.sqrt(spread + 1e-06) * norm_gain + norm_bias).astype(jnp.bfloat16)
    hidden = jnp.dot(normed, up_weight, preferred_element_type=jnp.float32) + up_bias
    hidden = jax.nn.gelu(hidden, approximate=False).astype(jnp.bfloat16)
    branch = jnp.dot(hidden, down_weight, preferred_element_type=jnp.float32) + down_bias
    result = x_tiles.reshape(-1, x_tiles.shape[-1]).astype(jnp.float32) + layer_scale * branch
    return result.astype(jnp.bfloat16).reshape(x_tiles.shape)

def depthwise_sum(padded, depth_kernel, depth_bias, rows, cols):
    total = jnp.zeros((rows, cols, padded.shape[2]), jnp.float32) + depth_bias
    for first in range(depth_kernel.shape[0]):
        for second in range(depth_kernel.shape[1]):
            window = padded[first:first + rows, second:second + cols].astype(jnp.float32)
            total = total + depth_kernel[first, second] * window
    return total.astype(jnp.bfloat16)

def reference(feature_map, depth_kernel, depth_bias, norm_gain, norm_bias, up_weight, up_bias, down_weight, down_bias, layer_scale, tile_route):
    half = KS // 2
    padded = jnp.pad(feature_map, ((half, half), (half, half), (0, 0)))
    depthwise = depthwise_sum(padded, depth_kernel, depth_bias, MAP_H, MAP_W)
    grid = DEV_GRID
    x_tiles = feature_map.reshape(GRID_Y, H_DEV, GRID_X, W_DEV, C).transpose(0, 2, 1, 3, 4).reshape(grid * H_DEV, W_DEV, C)
    dw_tiles = depthwise.reshape(GRID_Y, H_DEV, GRID_X, W_DEV, C).transpose(0, 2, 1, 3, 4).reshape(grid * H_DEV, W_DEV, C)
    incoming = tile_route.reshape(grid, grid, SLOT).transpose(1, 0, 2).reshape(grid, grid * SLOT)
    live = (incoming >= 0).astype(jnp.int32)
    rank = jnp.cumsum(live, axis=1) - 1
    slot_ids = jnp.arange(RECV, dtype=jnp.int32)
    select = ((rank[:, None, :] == slot_ids[None, :, None]) & (live[:, None, :] > 0)).astype(jnp.int32)
    positions = jnp.arange(grid * SLOT, dtype=jnp.int32)
    source = lax.optimization_barrier(jnp.sum(select * positions[None, None, :], axis=2)).astype(jnp.int32)
    valid = lax.optimization_barrier(jnp.sum(select, axis=2)) > 0
    entry = jnp.take_along_axis(incoming, source, axis=1)
    global_ids = (source // SLOT * H_DEV + jnp.maximum(entry, 0)).astype(jnp.int32)

    def one_receiver(args):
        ids, flags = args
        xs = jnp.take(x_tiles, ids, axis=0)
        ds = jnp.take(dw_tiles, ids, axis=0)
        result = pointwise(xs, ds, norm_gain, norm_bias, up_weight, up_bias, down_weight, down_bias, layer_scale)
        return jnp.where(flags[:, None, None], result, jnp.zeros_like(result))
    balanced = lax.map(one_receiver, (global_ids, valid))
    return balanced.reshape(grid * RECV, W_DEV, C)
```

```python
import functools

import jax
import jax.numpy as jnp
import numpy as np
from jax import lax
from jax.experimental import pallas as pl
from jax.experimental.pallas import tpu as pltpu
from jax.sharding import PartitionSpec as P

B16 = jnp.bfloat16
F32 = jnp.float32
MESH = pl.DeviceIdType.MESH
GY, GX = 4, 8
N = GY * GX
SLOT = 3
RECV = 48
ROWS, COLS, C = 128, 128, 256
HID = 1024
EXT = COLS + 16
KS = 7


def shift_matrix():
    s = np.zeros((COLS, KS * EXT), np.float32)
    for b in range(KS):
        for j in range(COLS):
            s[j, b * EXT + (j + b - 3) % EXT] = 1.0
    return s


def pack_matrices():
    first = np.zeros((64, 256), np.float32)
    last = np.zeros((64, 256), np.float32)
    for u in range(16):
        for c in range(4):
            first[u * 4 + c, u * 16 + c] = 1.0
            last[u * 4 + c, u * 16 + 12 + c] = 1.0
    return first, last


def unpack_matrices():
    left = np.zeros((256, 64), np.float32)
    right = np.zeros((256, 64), np.float32)
    for u in range(16):
        for c in range(3):
            right[u * 16 + c, u * 4 + c] = 1.0
            left[u * 16 + 13 + c, u * 4 + 1 + c] = 1.0
    return left, right


def corner_matrix():
    m = np.zeros((96, 64), np.float32)
    for r in range(3):
        for c in range(3):
            m[r * 16 + 13 + c, (r + 1) * 4 + 1 + c] = 1.0
            m[r * 16 + c, 16 + (r + 1) * 4 + c] = 1.0
            m[48 + r * 16 + 13 + c, 32 + r * 4 + 1 + c] = 1.0
            m[48 + r * 16 + c, 48 + r * 4 + c] = 1.0
    return m


def conv_tile(xp, kb, row, pp):
    for h in range(2):
        ls = slice(h * 128, (h + 1) * 128)
        for bs in ((0, 1, 2, 3), (4, 5, 6)):
            w = {(a, b): kb[a * KS + b, :, ls] for a in range(KS) for b in bs}

            def block(blk, _):
                o = pl.multiple_of(blk * 16, 16)
                xs = [xp[row + a, pl.ds(o, 16), ls] for a in range(KS)]
                for b in bs:
                    q = [xs[a] * w[(a, b)] for a in range(KS)]
                    s = ((q[0] + q[1]) + (q[2] + q[3])) + ((q[4] + q[5]) + q[6])
                    pp[pl.ds(b * EXT + o, 16), ls] = s
                return 0

            lax.fori_loop(0, EXT // 16, block, 0, unroll=True)


def order(k):
    i, j = k // GY, k % GY
    dy = jnp.where(j == 0, 2, jnp.where(j == 1, 1, jnp.where(j == 2, 3, 0)))
    half = (i + 1) // 2
    dx = (4 + jnp.where(i % 2 == 1, -half, half)) % GX
    return dy, dx


def block_kernel(
    route, x, sroute, kern, smat, pf, plast, ul, ur, cm, dbias, gain, nbias, uw, ub, dw, db, scale,
    recv, routes,
    xp, kb, pp, stage, hsend, hrecv, corner,
    xsem, rows_s, rows_r, cols_s, cols_r, cor_s, cor_r, rt_s, rt_r, send_s, recv_s, own_s,
):
    sl = lax.axis_index("slide")
    gy = lax.axis_index("gy")
    gx = lax.axis_index("gx")
    me = gy * GX + gx

    def dev(y, z):
        return (sl, y, z)

    load = pltpu.make_async_copy(x, xp.at[pl.ds(3, ROWS), pl.ds(0, COLS)], xsem)
    load.start()

    barrier = pltpu.get_barrier_semaphore()

    def greet(k, _):
        r = (me + 1 + k) % N
        pl.semaphore_signal(barrier, inc=1, device_id=dev(r // GX, r % GX), device_id_type=MESH)
        return 0

    lax.fori_loop(0, N - 1, greet, 0)

    def weights(i, _):
        kb[i] = jnp.broadcast_to(kern[i], (16, C)).astype(B16)
        return 0

    lax.fori_loop(0, KS * KS, weights, 0)
    load.wait()

    def pack(q, _):
        lo = xp[pl.ds(3 + q * 16, 16), 0:16, :].reshape(256, C)
        hi = xp[pl.ds(3 + q * 16, 16), COLS - 16 : COLS, :].reshape(256, C)
        hsend[0, q] = jnp.dot(pf[...], lo, preferred_element_type=F32).astype(B16)
        hsend[1, q] = jnp.dot(plast[...], hi, preferred_element_type=F32).astype(B16)
        return 0

    lax.fori_loop(0, 8, pack, 0)
    pl.semaphore_wait(barrier, N - 1)

    up, down = (gy + GY - 1) % GY, (gy + 1) % GY
    left, right = (gx + GX - 1) % GX, (gx + 1) % GX

    def remote(src, dst, s, r, where):
        return pltpu.make_async_remote_copy(
            src_ref=src, dst_ref=dst, send_sem=s, recv_sem=r, device_id=where, device_id_type=MESH
        )

    halo = [
        remote(hsend.at[0], hrecv.at[1], cols_s.at[0], cols_r.at[1], dev(gy, left)),
        remote(hsend.at[1], hrecv.at[0], cols_s.at[1], cols_r.at[0], dev(gy, right)),
        remote(x.at[pl.ds(0, 3)], xp.at[pl.ds(ROWS + 3, 3), pl.ds(0, COLS)], rows_s.at[0], rows_r.at[1], dev(up, gx)),
        remote(x.at[pl.ds(ROWS - 3, 3)], xp.at[pl.ds(0, 3), pl.ds(0, COLS)], rows_s.at[1], rows_r.at[0], dev(down, gx)),
        remote(hsend.at[1, 7, pl.ds(48, 16)], corner.at[pl.ds(0, 16)], cor_s.at[0], cor_r.at[0], dev(down, right)),
        remote(hsend.at[0, 7, pl.ds(48, 16)], corner.at[pl.ds(16, 16)], cor_s.at[1], cor_r.at[1], dev(down, left)),
        remote(hsend.at[1, 0, pl.ds(0, 16)], corner.at[pl.ds(32, 16)], cor_s.at[2], cor_r.at[2], dev(up, right)),
        remote(hsend.at[0, 0, pl.ds(0, 16)], corner.at[pl.ds(48, 16)], cor_s.at[3], cor_r.at[3], dev(up, left)),
    ]
    for h in halo:
        h.start()
    for h in halo:
        h.wait()

    @pl.when(gx == 0)
    def _():
        hrecv[0] = jnp.zeros_like(hrecv[0])
        corner[0:16] = jnp.zeros((16, C), B16)
        corner[32:48] = jnp.zeros((16, C), B16)

    @pl.when(gx == GX - 1)
    def _():
        hrecv[1] = jnp.zeros_like(hrecv[1])
        corner[16:32] = jnp.zeros((16, C), B16)
        corner[48:64] = jnp.zeros((16, C), B16)

    @pl.when(gy == 0)
    def _():
        xp[0:3, 0:COLS] = jnp.zeros((3, COLS, C), B16)
        corner[0:32] = jnp.zeros((32, C), B16)

    @pl.when(gy == GY - 1)
    def _():
        xp[ROWS + 3 : ROWS + 6, 0:COLS] = jnp.zeros((3, COLS, C), B16)
        corner[32:64] = jnp.zeros((32, C), B16)

    def unpack(q, _):
        both = jnp.dot(ul[...], hrecv[0, q], preferred_element_type=F32) + jnp.dot(
            ur[...], hrecv[1, q], preferred_element_type=F32
        )
        xp[pl.ds(3 + q * 16, 16), COLS:EXT, :] = both.astype(B16).reshape(16, 16, C)
        return 0

    lax.fori_loop(0, 8, unpack, 0)
    edge = jnp.dot(cm[...], corner[...], preferred_element_type=F32).astype(B16).reshape(2, 3, 16, C)
    xp[0:3, COLS:EXT, :] = edge[0]
    xp[ROWS + 3 : ROWS + 6, COLS:EXT, :] = edge[1]

    def place(k):
        dy, dx = order(k)
        return (gy + dy) % GY, (gx + dx) % GX

    def tell(k, _):
        ry, rx = place(k)
        remote(sroute.at[ry * GX + rx], routes.at[me], rt_s, rt_r, dev(ry, rx)).start()
        return 0

    lax.fori_loop(0, N - 1, tell, 0)

    def compute(k):
        ry, rx = place(k)
        r = ry * GX + rx
        rows = [jnp.maximum(route[0, r * SLOT + t], 0) for t in range(SLOT)]
        normed = []
        for t in range(SLOT):
            conv_tile(xp, kb, rows[t], pp.at[t])
        for t in range(SLOT):
            d = jnp.dot(smat[...], pp[t], preferred_element_type=F32) + dbias[...]
            c = d - jnp.mean(d, axis=1, keepdims=True)
            v = jnp.mean(c * c, axis=1, keepdims=True)
            normed.append((c * lax.rsqrt(v + 1e-6) * gain[...] + nbias[...]).astype(B16))
        n = jnp.concatenate(normed, axis=0)
        branch = None
        for q in range(4):
            qs = slice(q * 256, (q + 1) * 256)
            hh = jnp.dot(n, uw[:, qs], preferred_element_type=F32) + ub[:, qs]
            g = (0.5 * hh * (1.0 + lax.erf(hh * 0.7071067811865476))).astype(B16)
            part = jnp.dot(g, dw[qs, :], preferred_element_type=F32)
            branch = part if branch is None else branch + part
        branch = branch + db[...]
        for t in range(SLOT):
            o = xp[rows[t] + 3, 0:COLS, :].astype(F32) + scale[...] * branch[t * COLS : (t + 1) * COLS]
            stage[k, t] = o.astype(B16)
        return ry, rx

    def step(k, _):
        ry, rx = compute(k)

        @pl.when(k < N - 1)
        def _():
            remote(stage.at[k], recv.at[me], send_s.at[k], recv_s.at[me], dev(ry, rx)).start()

        @pl.when(k == N - 1)
        def _():
            pltpu.make_async_copy(stage.at[k], recv.at[me], own_s.at[0]).start()

        return 0

    lax.fori_loop(0, N, step, 0)
    mine = pltpu.make_async_copy(sroute.at[me], routes.at[me], own_s.at[1])
    mine.start()
    mine.wait()
    pltpu.make_async_copy(stage.at[N - 1], recv.at[me], own_s.at[0]).wait()
    several = routes.at[pl.ds(0, N - 1)]
    pltpu.make_async_copy(several, several, rt_s).wait()
    pltpu.make_async_copy(several, several, rt_r).wait()

    def finish(k, _):
        s = (me + 1 + k) % N
        here = remote(stage.at[k], recv.at[s], send_s.at[k], recv_s.at[s], dev(gy, gx))
        here.wait_send()
        here.wait_recv()
        return 0

    lax.fori_loop(0, N - 1, finish, 0)


def compact_kernel(routes, recv, out, zero, sem):
    zero[...] = jnp.zeros_like(zero)

    def look(i, count):
        v = routes[i // SLOT, 0, i % SLOT]
        take = jnp.logical_and(v >= 0, count < RECV)

        @pl.when(take)
        def _():
            pltpu.make_async_copy(recv.at[i // SLOT, i % SLOT], out.at[count], sem).start()

        return count + take.astype(jnp.int32)

    count = lax.fori_loop(0, N * SLOT, look, jnp.int32(0))

    def blank(k, _):
        pltpu.make_async_copy(zero, out.at[k], sem).start()
        return 0

    lax.fori_loop(count, RECV, blank, 0)
    pltpu.make_async_copy(out, out, sem).wait()


def per_device(
    feature_map, depth_kernel, depth_bias, norm_gain, norm_bias, up_weight, up_bias, down_weight, down_bias,
    layer_scale, tile_route,
):
    vm = pl.BlockSpec(memory_space=pltpu.VMEM)
    anym = pl.BlockSpec(memory_space=pl.ANY)
    smem = pl.BlockSpec(memory_space=pltpu.SMEM)
    sroute = jnp.pad(tile_route.reshape(N, 1, SLOT), ((0, 0), (0, 0), (0, 128 - SLOT)), constant_values=-1)
    pf, plast = pack_matrices()
    ul, ur = unpack_matrices()
    const = [jnp.asarray(m, B16) for m in (shift_matrix(), pf, plast, ul, ur, corner_matrix())]
    row = lambda a: a.reshape(1, -1)
    dma = pltpu.SemaphoreType.DMA
    recv, routes = pl.pallas_call(
        block_kernel,
        out_shape=(
            jax.ShapeDtypeStruct((N, SLOT, COLS, C), B16),
            jax.ShapeDtypeStruct((N, 1, 128), jnp.int32),
        ),
        in_specs=[smem, anym, anym] + [vm] * 15,
        out_specs=(anym, anym),
        scratch_shapes=[
            pltpu.VMEM((ROWS + 6, EXT, C), B16),
            pltpu.VMEM((KS * KS, 16, C), B16),
            pltpu.VMEM((SLOT, KS * EXT, C), B16),
            pltpu.VMEM((N, SLOT, COLS, C), B16),
            pltpu.VMEM((2, 8, 64, C), B16),
            pltpu.VMEM((2, 8, 64, C), B16),
            pltpu.VMEM((64, C), B16),
            dma,
            dma((2,)), dma((2,)), dma((2,)), dma((2,)), dma((4,)), dma((4,)),
            dma, dma, dma((N,)), dma((N,)), dma((2,)),
        ],
        compiler_params=pltpu.CompilerParams(
            collective_id=0, has_side_effects=True, vmem_limit_bytes=56 * 2**20
        ),
    )(
        tile_route, feature_map, sroute, depth_kernel.reshape(KS * KS, 1, C), *const, row(depth_bias),
        row(norm_gain), row(norm_bias), up_weight, row(up_bias), down_weight, row(down_bias), row(layer_scale),
    )
    return pl.pallas_call(
        compact_kernel,
        out_shape=jax.ShapeDtypeStruct((RECV, COLS, C), B16),
        in_specs=[smem, anym],
        out_specs=anym,
        scratch_shapes=[pltpu.VMEM((COLS, C), B16), dma],
    )(routes, recv)


def solution(mesh):
    in_specs = (P(("slide", "gy"), "gx", None),) + (P(),) * 9 + (P(("slide", "gy", "gx"), None),)
    out_specs = P(("slide", "gy", "gx"), None, None)
    return jax.shard_map(per_device, mesh=mesh, in_specs=in_specs, out_specs=out_specs, check_vma=False)
```

```python
import functools

import jax
import jax.numpy as jnp
import numpy as np
from jax import lax
from jax.experimental import pallas as pl
from jax.experimental.pallas import tpu as pltpu
from jax.sharding import PartitionSpec as P

B16 = jnp.bfloat16
F32 = jnp.float32
MESH = pl.DeviceIdType.MESH
GY, GX = 4, 8
N = GY * GX
SLOT = 3
RECV = 48
ROWS, COLS, C = 128, 128, 256
HID = 1024
EXT = COLS + 16
KS = 7


def shift_matrix():
    s = np.zeros((COLS, KS * EXT), np.float32)
    for b in range(KS):
        for j in range(COLS):
            s[j, b * EXT + (j + b - 3) % EXT] = 1.0
    return s


def pack_matrices():
    first = np.zeros((64, 256), np.float32)
    last = np.zeros((64, 256), np.float32)
    for u in range(16):
        for c in range(4):
            first[u * 4 + c, u * 16 + c] = 1.0
            last[u * 4 + c, u * 16 + 12 + c] = 1.0
    return first, last


def unpack_matrices():
    left = np.zeros((256, 64), np.float32)
    right = np.zeros((256, 64), np.float32)
    for u in range(16):
        for c in range(3):
            right[u * 16 + c, u * 4 + c] = 1.0
            left[u * 16 + 13 + c, u * 4 + 1 + c] = 1.0
    return left, right


def corner_matrix():
    m = np.zeros((96, 64), np.float32)
    for r in range(3):
        for c in range(3):
            m[r * 16 + 13 + c, (r + 1) * 4 + 1 + c] = 1.0
            m[r * 16 + c, 16 + (r + 1) * 4 + c] = 1.0
            m[48 + r * 16 + 13 + c, 32 + r * 4 + 1 + c] = 1.0
            m[48 + r * 16 + c, 48 + r * 4 + c] = 1.0
    return m


GROUPS = ((0, 1, 2), (3, 4), (5, 6))
STEPS = (
    (2, 2), (1, 1), (3, 3), (2, 0), (0, 2), (1, 3), (3, 1), (2, 1),
    (1, 0), (2, 3), (3, 0), (1, 2), (0, 1), (3, 2), (0, 3), (0, 0),
)


def conv_group(xp, kb, rows, pp):
    for bs in GROUPS:
        w = {(a, b): kb[a * KS + b] for a in range(KS) for b in bs}

        def block(blk, _):
            o = pl.multiple_of(blk * 16, 16)
            for t, row in enumerate(rows):
                xs = [xp[row + a, pl.ds(o, 16), :] for a in range(KS)]
                for b in bs:
                    q = [xs[a] * w[(a, b)] for a in range(KS)]
                    s = ((q[0] + q[1]) + (q[2] + q[3])) + ((q[4] + q[5]) + q[6])
                    pp[t, pl.ds(b * EXT + o, 16), :] = s
            return 0

        lax.fori_loop(0, EXT // 16, block, 0)


def look_up(k, table):
    return sum(jnp.where(k == i, v, 0) for i, v in enumerate(table))


def block_kernel(
    route, x, sroute, kern, smat, pf, plast, ul, ur, cm, dbias, gain, nbias, uw, ub, dw, db, scale,
    recv, routes,
    xp, kb, pp, stage, hsend, hrecv, corner,
    xsem, rows_s, rows_r, cols_s, cols_r, cor_s, cor_r, rt_s, rt_r, send_s, recv_s, own_s,
):
    sl = lax.axis_index("slide")
    gy = lax.axis_index("gy")
    gx = lax.axis_index("gx")
    me = gy * GX + gx

    def dev(y, z):
        return (sl, y, z)

    load = pltpu.make_async_copy(x, xp.at[pl.ds(3, ROWS), pl.ds(0, COLS)], xsem)
    load.start()

    barrier = pltpu.get_barrier_semaphore()

    def greet(k, _):
        r = (me + 1 + k) % N
        pl.semaphore_signal(barrier, inc=1, device_id=dev(r // GX, r % GX), device_id_type=MESH)
        return 0

    lax.fori_loop(0, N - 1, greet, 0)

    for a in range(KS):
        for b in range(KS):
            kb[a * KS + b] = jnp.broadcast_to(kern[a, b : b + 1, :], (16, C)).astype(B16)

    up, down = (gy + GY - 1) % GY, (gy + 1) % GY
    left, right = (gx + GX - 1) % GX, (gx + 1) % GX

    def remote(src, dst, s, r, where):
        return pltpu.make_async_remote_copy(
            src_ref=src, dst_ref=dst, send_sem=s, recv_sem=r, device_id=where, device_id_type=MESH
        )

    halo_rows = [
        remote(x.at[pl.ds(0, 3)], xp.at[pl.ds(ROWS + 3, 3), pl.ds(0, COLS)], rows_s.at[0], rows_r.at[1], dev(up, gx)),
        remote(x.at[pl.ds(ROWS - 3, 3)], xp.at[pl.ds(0, 3), pl.ds(0, COLS)], rows_s.at[1], rows_r.at[0], dev(down, gx)),
    ]
    halo_cols = [
        remote(hsend.at[0], hrecv.at[1], cols_s.at[0], cols_r.at[1], dev(gy, left)),
        remote(hsend.at[1], hrecv.at[0], cols_s.at[1], cols_r.at[0], dev(gy, right)),
        remote(hsend.at[1, 7, pl.ds(48, 16)], corner.at[pl.ds(0, 16)], cor_s.at[0], cor_r.at[0], dev(down, right)),
        remote(hsend.at[0, 7, pl.ds(48, 16)], corner.at[pl.ds(16, 16)], cor_s.at[1], cor_r.at[1], dev(down, left)),
        remote(hsend.at[1, 0, pl.ds(0, 16)], corner.at[pl.ds(32, 16)], cor_s.at[2], cor_r.at[2], dev(up, right)),
        remote(hsend.at[0, 0, pl.ds(0, 16)], corner.at[pl.ds(48, 16)], cor_s.at[3], cor_r.at[3], dev(up, left)),
    ]

    pl.semaphore_wait(barrier, N - 1)
    for h in halo_rows:
        h.start()
    load.wait()
    for q in range(8):
        lo = xp[3 + q * 16 : 19 + q * 16, 0:16, :].reshape(256, C)
        hi = xp[3 + q * 16 : 19 + q * 16, COLS - 16 : COLS, :].reshape(256, C)
        hsend[0, q] = jnp.dot(pf[...], lo, preferred_element_type=F32).astype(B16)
        hsend[1, q] = jnp.dot(plast[...], hi, preferred_element_type=F32).astype(B16)
    for h in halo_cols:
        h.start()

    def place(k):
        core, cx = gx % 2, gx // 2
        c, t = k // 2, k % 2
        a, b = look_up(c, [o[0] for o in STEPS]), look_up(c, [o[1] for o in STEPS])
        dy, dx = jnp.where(core == 0, a, b), jnp.where(core == 0, b, a)
        return (gy + dy) % GY, ((cx + dx) % (GX // 2)) * 2 + (core + 1 + t) % 2

    def tell(k, _):
        ry, rx = place(k)
        remote(sroute, routes.at[me], rt_s, rt_r, dev(ry, rx)).start()
        return 0

    lax.fori_loop(0, N - 1, tell, 0)
    mine = pltpu.make_async_copy(sroute, routes.at[me], own_s.at[1])
    mine.start()

    for h in halo_cols:
        h.wait()

    @pl.when(gx == 0)
    def _():
        hrecv[0] = jnp.zeros_like(hrecv[0])
        corner[0:16] = jnp.zeros((16, C), B16)
        corner[32:48] = jnp.zeros((16, C), B16)

    @pl.when(gx == GX - 1)
    def _():
        hrecv[1] = jnp.zeros_like(hrecv[1])
        corner[16:32] = jnp.zeros((16, C), B16)
        corner[48:64] = jnp.zeros((16, C), B16)

    @pl.when(gy == 0)
    def _():
        corner[0:32] = jnp.zeros((32, C), B16)

    @pl.when(gy == GY - 1)
    def _():
        corner[32:64] = jnp.zeros((32, C), B16)

    for q in range(8):
        both = jnp.dot(ul[...], hrecv[0, q], preferred_element_type=F32) + jnp.dot(
            ur[...], hrecv[1, q], preferred_element_type=F32
        )
        xp[3 + q * 16 : 19 + q * 16, COLS:EXT, :] = both.astype(B16).reshape(16, 16, C)
    edge = jnp.dot(cm[...], corner[...], preferred_element_type=F32).astype(B16).reshape(2, 3, 16, C)
    xp[0:3, COLS:EXT, :] = edge[0]
    xp[ROWS + 3 : ROWS + 6, COLS:EXT, :] = edge[1]

    for h in halo_rows:
        h.wait()

    @pl.when(gy == 0)
    def _():
        xp[0:3, 0:COLS] = jnp.zeros((3, COLS, C), B16)

    @pl.when(gy == GY - 1)
    def _():
        xp[ROWS + 3 : ROWS + 6, 0:COLS] = jnp.zeros((3, COLS, C), B16)

    def compute(k):
        ry, rx = place(k)
        r = ry * GX + rx
        rows = [jnp.maximum(route[0, r * SLOT + t], 0) for t in range(SLOT)]
        normed = []
        conv_group(xp, kb, rows, pp)
        for t in range(SLOT):
            d = jnp.dot(smat[...], pp[t], preferred_element_type=F32) + dbias[...]
            c = d - jnp.mean(d, axis=1, keepdims=True)
            v = jnp.mean(c * c, axis=1, keepdims=True)
            normed.append((c * lax.rsqrt(v + 1e-6) * gain[...] + nbias[...]).astype(B16))
        n = jnp.concatenate(normed, axis=0)
        branch = None
        for q in range(4):
            qs = slice(q * 256, (q + 1) * 256)
            hh = jnp.dot(n, uw[:, qs], preferred_element_type=F32) + ub[:, qs]
            g = (0.5 * hh * (1.0 + lax.erf(hh * 0.7071067811865476))).astype(B16)
            part = jnp.dot(g, dw[qs, :], preferred_element_type=F32)
            branch = part if branch is None else branch + part
        branch = branch + db[...]
        for t in range(SLOT):
            o = xp[rows[t] + 3, 0:COLS, :].astype(F32) + scale[...] * branch[t * COLS : (t + 1) * COLS]
            stage[k, t] = o.astype(B16)
        return ry, rx

    def step(k, _):
        ry, rx = compute(k)

        @pl.when(k < N - 1)
        def _():
            remote(stage.at[k], recv.at[me], send_s.at[k], recv_s.at[me], dev(ry, rx)).start()

        @pl.when(k == N - 1)
        def _():
            pltpu.make_async_copy(stage.at[k], recv.at[me], own_s.at[0]).start()

        return 0

    lax.fori_loop(0, N, step, 0)
    mine.wait()
    pltpu.make_async_copy(stage.at[N - 1], recv.at[me], own_s.at[0]).wait()
    several = routes.at[pl.ds(0, N - 1)]
    pltpu.make_async_copy(several, several, rt_s).wait()
    pltpu.make_async_copy(several, several, rt_r).wait()

    def finish(k, _):
        s = (me + 1 + k) % N
        here = remote(stage.at[k], recv.at[s], send_s.at[k], recv_s.at[s], dev(gy, gx))
        here.wait_send()
        here.wait_recv()
        return 0

    lax.fori_loop(0, N - 1, finish, 0)


def compact_kernel(routes, recv, out, held, in_s, out_s):
    me = lax.axis_index("gy") * GX + lax.axis_index("gx")

    def look(i, count):
        v = routes[i // SLOT, 0, me * SLOT + i % SLOT]
        take = jnp.logical_and(v >= 0, count < RECV)

        @pl.when(take)
        def _():
            pltpu.make_async_copy(recv.at[i // SLOT, i % SLOT], held.at[count], in_s.at[count]).start()

        return count + take.astype(jnp.int32)

    count = lax.fori_loop(0, N * SLOT, look, jnp.int32(0))

    def blank(k, _):
        held[k] = jnp.zeros((COLS, C), B16)
        return 0

    lax.fori_loop(count, RECV, blank, 0)

    def pass_on(k, _):
        @pl.when(k < count)
        def _():
            pltpu.make_async_copy(recv.at[0, 0], held.at[k], in_s.at[k]).wait()

        pltpu.make_async_copy(held.at[k], out.at[k], out_s).start()
        return 0

    lax.fori_loop(0, RECV, pass_on, 0)
    pltpu.make_async_copy(held, out, out_s).wait()


def per_device(
    feature_map, depth_kernel, depth_bias, norm_gain, norm_bias, up_weight, up_bias, down_weight, down_bias,
    layer_scale, tile_route,
):
    vm = pl.BlockSpec(memory_space=pltpu.VMEM)
    anym = pl.BlockSpec(memory_space=pl.ANY)
    smem = pl.BlockSpec(memory_space=pltpu.SMEM)
    pf, plast = pack_matrices()
    ul, ur = unpack_matrices()
    const = [jnp.asarray(m, B16) for m in (shift_matrix(), pf, plast, ul, ur, corner_matrix())]
    row = lambda a: a.reshape(1, -1)
    dma = pltpu.SemaphoreType.DMA
    recv, routes = pl.pallas_call(
        block_kernel,
        out_shape=(
            jax.ShapeDtypeStruct((N, SLOT, COLS, C), B16),
            jax.ShapeDtypeStruct((N, 1, N * SLOT), jnp.int32),
        ),
        in_specs=[smem, anym, anym] + [vm] * 15,
        out_specs=(anym, anym),
        scratch_shapes=[
            pltpu.VMEM((ROWS + 6, EXT, C), B16),
            pltpu.VMEM((KS * KS, 16, C), B16),
            pltpu.VMEM((SLOT, KS * EXT, C), B16),
            pltpu.VMEM((N, SLOT, COLS, C), B16),
            pltpu.VMEM((2, 8, 64, C), B16),
            pltpu.VMEM((2, 8, 64, C), B16),
            pltpu.VMEM((64, C), B16),
            dma,
            dma((2,)), dma((2,)), dma((2,)), dma((2,)), dma((4,)), dma((4,)),
            dma, dma, dma((N,)), dma((N,)), dma((2,)),
        ],
        compiler_params=pltpu.CompilerParams(
            collective_id=0, has_side_effects=True, vmem_limit_bytes=56 * 2**20
        ),
    )(
        tile_route, feature_map, tile_route, depth_kernel, *const, row(depth_bias),
        row(norm_gain), row(norm_bias), up_weight, row(up_bias), down_weight, row(down_bias), row(layer_scale),
    )
    return pl.pallas_call(
        compact_kernel,
        out_shape=jax.ShapeDtypeStruct((RECV, COLS, C), B16),
        in_specs=[smem, anym],
        out_specs=anym,
        scratch_shapes=[pltpu.VMEM((RECV, COLS, C), B16), dma((RECV,)), dma],
    )(routes, recv)


def solution(mesh):
    in_specs = (P(("slide", "gy"), "gx", None),) + (P(),) * 9 + (P(("slide", "gy", "gx"), None),)
    out_specs = P(("slide", "gy", "gx"), None, None)
    return jax.shard_map(per_device, mesh=mesh, in_specs=in_specs, out_specs=out_specs, check_vma=False)
```

```python
import functools

import jax
import jax.numpy as jnp
import numpy as np
from jax import lax
from jax.experimental import pallas as pl
from jax.experimental.pallas import tpu as pltpu
from jax.sharding import PartitionSpec as P

B16 = jnp.bfloat16
F32 = jnp.float32
MESH = pl.DeviceIdType.MESH
GY, GX = 4, 8
N = GY * GX
SLOT = 3
RECV = 48
ROWS, COLS, C = 128, 128, 256
HID = 1024
EXT = COLS + 16
KS = 7


def shift_matrix():
    s = np.zeros((COLS, KS * EXT), np.float32)
    for b in range(KS):
        for j in range(COLS):
            s[j, b * EXT + (j + b - 3) % EXT] = 1.0
    return s


def pack_matrices():
    first = np.zeros((64, 256), np.float32)
    last = np.zeros((64, 256), np.float32)
    for u in range(16):
        for c in range(4):
            first[u * 4 + c, u * 16 + c] = 1.0
            last[u * 4 + c, u * 16 + 12 + c] = 1.0
    return first, last


def unpack_matrices():
    left = np.zeros((256, 64), np.float32)
    right = np.zeros((256, 64), np.float32)
    for u in range(16):
        for c in range(3):
            right[u * 16 + c, u * 4 + c] = 1.0
            left[u * 16 + 13 + c, u * 4 + 1 + c] = 1.0
    return left, right


def corner_matrix():
    m = np.zeros((96, 64), np.float32)
    for r in range(3):
        for c in range(3):
            m[r * 16 + 13 + c, (r + 1) * 4 + 1 + c] = 1.0
            m[r * 16 + c, 16 + (r + 1) * 4 + c] = 1.0
            m[48 + r * 16 + 13 + c, 32 + r * 4 + 1 + c] = 1.0
            m[48 + r * 16 + c, 48 + r * 4 + c] = 1.0
    return m


GROUPS = ((0, 1, 2), (3, 4), (5, 6))
CHIPS = (
    (2, 2), (1, 1), (3, 3), (2, 0), (0, 2), (1, 3), (3, 1), (2, 1),
    (1, 0), (2, 3), (3, 0), (1, 2), (0, 1), (3, 2), (0, 3),
)
STEPS = tuple(
    sorted(
        [(z, x, t) for t in (1, 0) for z, x in CHIPS],
        key=lambda o: -(o[0] == 2) - (o[1] == 2),
    )
) + ((0, 0, 1), (0, 0, 0))


def conv_group(xp, kb, rows, pp):
    for bs in GROUPS:
        w = {(a, b): kb[a * KS + b] for a in range(KS) for b in bs}

        def block(blk, _):
            o = pl.multiple_of(blk * 16, 16)
            for t, row in enumerate(rows):
                xs = [xp[row + a, pl.ds(o, 16), :] for a in range(KS)]
                for b in bs:
                    q = [xs[a] * w[(a, b)] for a in range(KS)]
                    s = ((q[0] + q[1]) + (q[2] + q[3])) + ((q[4] + q[5]) + q[6])
                    pp[t, pl.ds(b * EXT + o, 16), :] = s
            return 0

        lax.fori_loop(0, EXT // 16, block, 0)


def look_up(k, table):
    return sum(jnp.where(k == i, v, 0) for i, v in enumerate(table))


def block_kernel(
    route, x, sroute, kern, smat_h, pf, plast, ul, ur, cm, dbias, gain, nbias, uw_h, ub, dw_h, db, scale,
    recv, routes,
    xp, kb, pp, stage, hsend, hrecv, corner, smat, uw, dw,
    xsem, rows_s, rows_r, cols_s, cols_r, cor_s, cor_r, rt_s, rt_r, send_s, recv_s, own_s, w_s,
):
    sl = lax.axis_index("slide")
    gy = lax.axis_index("gy")
    gx = lax.axis_index("gx")
    me = gy * GX + gx

    def dev(y, z):
        return (sl, y, z)

    load = pltpu.make_async_copy(x, xp.at[pl.ds(3, ROWS), pl.ds(0, COLS)], xsem)
    load.start()

    barrier = pltpu.get_barrier_semaphore()

    def greet(k, _):
        r = (me + 1 + k) % N
        pl.semaphore_signal(barrier, inc=1, device_id=dev(r // GX, r % GX), device_id_type=MESH)
        return 0

    lax.fori_loop(0, N - 1, greet, 0)
    held = [
        pltpu.make_async_copy(h, v, w_s.at[i]) for i, (h, v) in enumerate(((smat_h, smat), (uw_h, uw), (dw_h, dw)))
    ]
    for h in held:
        h.start()

    for a in range(KS):
        for b in range(KS):
            kb[a * KS + b] = jnp.broadcast_to(kern[a, b : b + 1, :], (16, C)).astype(B16)

    up, down = (gy + GY - 1) % GY, (gy + 1) % GY
    left, right = (gx + GX - 1) % GX, (gx + 1) % GX

    def remote(src, dst, s, r, where):
        return pltpu.make_async_remote_copy(
            src_ref=src, dst_ref=dst, send_sem=s, recv_sem=r, device_id=where, device_id_type=MESH
        )

    halo_rows = [
        remote(x.at[pl.ds(0, 3)], xp.at[pl.ds(ROWS + 3, 3), pl.ds(0, COLS)], rows_s.at[0], rows_r.at[1], dev(up, gx)),
        remote(x.at[pl.ds(ROWS - 3, 3)], xp.at[pl.ds(0, 3), pl.ds(0, COLS)], rows_s.at[1], rows_r.at[0], dev(down, gx)),
    ]
    halo_cols = [
        remote(hsend.at[0], hrecv.at[1], cols_s.at[0], cols_r.at[1], dev(gy, left)),
        remote(hsend.at[1], hrecv.at[0], cols_s.at[1], cols_r.at[0], dev(gy, right)),
        remote(hsend.at[1, 7, pl.ds(48, 16)], corner.at[pl.ds(0, 16)], cor_s.at[0], cor_r.at[0], dev(down, right)),
        remote(hsend.at[0, 7, pl.ds(48, 16)], corner.at[pl.ds(16, 16)], cor_s.at[1], cor_r.at[1], dev(down, left)),
        remote(hsend.at[1, 0, pl.ds(0, 16)], corner.at[pl.ds(32, 16)], cor_s.at[2], cor_r.at[2], dev(up, right)),
        remote(hsend.at[0, 0, pl.ds(0, 16)], corner.at[pl.ds(48, 16)], cor_s.at[3], cor_r.at[3], dev(up, left)),
    ]

    pl.semaphore_wait(barrier, N - 1)
    for h in halo_rows:
        h.start()
    load.wait()
    for q in range(8):
        lo = xp[3 + q * 16 : 19 + q * 16, 0:16, :].reshape(256, C)
        hi = xp[3 + q * 16 : 19 + q * 16, COLS - 16 : COLS, :].reshape(256, C)
        hsend[0, q] = jnp.dot(pf[...], lo, preferred_element_type=F32).astype(B16)
        hsend[1, q] = jnp.dot(plast[...], hi, preferred_element_type=F32).astype(B16)
    for h in halo_cols:
        h.start()

    def place(k):
        core, cx = gx % 2, gx // 2
        a, b, t = (look_up(k, [o[i] for o in STEPS]) for i in range(3))
        dy, dx = jnp.where(core == 0, a, b), jnp.where(core == 0, b, a)
        return (gy + dy) % GY, ((cx + dx) % (GX // 2)) * 2 + (core + t) % 2

    def tell(k, _):
        ry, rx = place(k)
        remote(sroute, routes.at[me], rt_s, rt_r, dev(ry, rx)).start()
        return 0

    lax.fori_loop(0, N - 1, tell, 0)
    mine = pltpu.make_async_copy(sroute, routes.at[me], own_s.at[1])
    mine.start()

    for h in halo_cols:
        h.wait()

    @pl.when(gx == 0)
    def _():
        hrecv[0] = jnp.zeros_like(hrecv[0])
        corner[0:16] = jnp.zeros((16, C), B16)
        corner[32:48] = jnp.zeros((16, C), B16)

    @pl.when(gx == GX - 1)
    def _():
        hrecv[1] = jnp.zeros_like(hrecv[1])
        corner[16:32] = jnp.zeros((16, C), B16)
        corner[48:64] = jnp.zeros((16, C), B16)

    @pl.when(gy == 0)
    def _():
        corner[0:32] = jnp.zeros((32, C), B16)

    @pl.when(gy == GY - 1)
    def _():
        corner[32:64] = jnp.zeros((32, C), B16)

    for q in range(8):
        both = jnp.dot(ul[...], hrecv[0, q], preferred_element_type=F32) + jnp.dot(
            ur[...], hrecv[1, q], preferred_element_type=F32
        )
        xp[3 + q * 16 : 19 + q * 16, COLS:EXT, :] = both.astype(B16).reshape(16, 16, C)
    edge = jnp.dot(cm[...], corner[...], preferred_element_type=F32).astype(B16).reshape(2, 3, 16, C)
    xp[0:3, COLS:EXT, :] = edge[0]
    xp[ROWS + 3 : ROWS + 6, COLS:EXT, :] = edge[1]

    for h in halo_rows:
        h.wait()

    @pl.when(gy == 0)
    def _():
        xp[0:3, 0:COLS] = jnp.zeros((3, COLS, C), B16)

    @pl.when(gy == GY - 1)
    def _():
        xp[ROWS + 3 : ROWS + 6, 0:COLS] = jnp.zeros((3, COLS, C), B16)

    for h in held:
        h.wait()

    def compute(k):
        ry, rx = place(k)
        r = ry * GX + rx
        rows = [jnp.maximum(route[0, r * SLOT + t], 0) for t in range(SLOT)]
        normed = []
        conv_group(xp, kb, rows, pp)
        for t in range(SLOT):
            d = jnp.dot(smat[...], pp[t], preferred_element_type=F32) + dbias[...]
            c = d - jnp.mean(d, axis=1, keepdims=True)
            v = jnp.mean(c * c, axis=1, keepdims=True)
            normed.append((c * lax.rsqrt(v + 1e-6) * gain[...] + nbias[...]).astype(B16))
        n = jnp.concatenate(normed, axis=0)
        branch = None
        for q in range(4):
            qs = slice(q * 256, (q + 1) * 256)
            hh = jnp.dot(n, uw[:, qs], preferred_element_type=F32) + ub[:, qs]
            g = (0.5 * hh * (1.0 + lax.erf(hh * 0.7071067811865476))).astype(B16)
            part = jnp.dot(g, dw[qs, :], preferred_element_type=F32)
            branch = part if branch is None else branch + part
        branch = branch + db[...]
        for t in range(SLOT):
            o = xp[rows[t] + 3, 0:COLS, :].astype(F32) + scale[...] * branch[t * COLS : (t + 1) * COLS]
            stage[k, t] = o.astype(B16)
        return ry, rx

    def step(k, _):
        ry, rx = compute(k)

        @pl.when(k < N - 1)
        def _():
            remote(stage.at[k], recv.at[me], send_s, recv_s, dev(ry, rx)).start()

        @pl.when(k == N - 1)
        def _():
            pltpu.make_async_copy(stage.at[k], recv.at[me], own_s.at[0]).start()

        return 0

    lax.fori_loop(0, N, step, 0)
    mine.wait()
    pltpu.make_async_copy(stage.at[N - 1], recv.at[me], own_s.at[0]).wait()
    several = routes.at[pl.ds(0, N - 1)]
    pltpu.make_async_copy(several, several, rt_s).wait()
    pltpu.make_async_copy(several, several, rt_r).wait()

    sent = stage.at[pl.ds(0, N - 1)]
    pltpu.make_async_copy(sent, sent, send_s).wait()
    pltpu.make_async_copy(sent, sent, recv_s).wait()


def compact_kernel(routes, recv, out, zero, sem):
    me = lax.axis_index("gy") * GX + lax.axis_index("gx")
    zero[...] = jnp.zeros_like(zero)

    def look(i, count):
        g, s = i // SLOT, i % SLOT
        take = jnp.logical_and(routes[g, 0, me * SLOT + s] >= 0, count < RECV)

        @pl.when(take)
        def _():
            pltpu.make_async_copy(recv.at[g, s], out.at[count], sem).start()

        return count + take.astype(jnp.int32)

    count = lax.fori_loop(0, N * SLOT, look, jnp.int32(0))

    def blank(k, _):
        pltpu.make_async_copy(zero, out.at[k], sem).start()
        return 0

    lax.fori_loop(count, RECV, blank, 0)
    pltpu.make_async_copy(out, out, sem).wait()


def per_device(
    feature_map, depth_kernel, depth_bias, norm_gain, norm_bias, up_weight, up_bias, down_weight, down_bias,
    layer_scale, tile_route,
):
    vm = pl.BlockSpec(memory_space=pltpu.VMEM)
    anym = pl.BlockSpec(memory_space=pl.ANY)
    smem = pl.BlockSpec(memory_space=pltpu.SMEM)
    pf, plast = pack_matrices()
    ul, ur = unpack_matrices()
    const = [jnp.asarray(m, B16) for m in (shift_matrix(), pf, plast, ul, ur, corner_matrix())]
    row = lambda a: a.reshape(1, -1)
    dma = pltpu.SemaphoreType.DMA
    recv, routes = pl.pallas_call(
        block_kernel,
        out_shape=(
            pltpu.VMEM((N, SLOT, COLS, C), B16),
            jax.ShapeDtypeStruct((N, 1, N * SLOT), jnp.int32),
        ),
        in_specs=[smem, anym, anym, vm, anym] + [vm] * 8 + [anym, vm, anym, vm, vm],
        out_specs=(vm, anym),
        scratch_shapes=[
            pltpu.VMEM((ROWS + 6, EXT, C), B16),
            pltpu.VMEM((KS * KS, 16, C), B16),
            pltpu.VMEM((SLOT, KS * EXT, C), B16),
            pltpu.VMEM((N, SLOT, COLS, C), B16),
            pltpu.VMEM((2, 8, 64, C), B16),
            pltpu.VMEM((2, 8, 64, C), B16),
            pltpu.VMEM((64, C), B16),
            pltpu.VMEM((COLS, KS * EXT), B16),
            pltpu.VMEM((C, HID), B16),
            pltpu.VMEM((HID, C), B16),
            dma,
            dma((2,)), dma((2,)), dma((2,)), dma((2,)), dma((4,)), dma((4,)),
            dma, dma, dma, dma, dma((2,)), dma((3,)),
        ],
        compiler_params=pltpu.CompilerParams(
            collective_id=0, has_side_effects=True, vmem_limit_bytes=50 * 2**20
        ),
    )(
        tile_route, feature_map, tile_route, depth_kernel, *const, row(depth_bias),
        row(norm_gain), row(norm_bias), up_weight, row(up_bias), down_weight, row(down_bias), row(layer_scale),
    )
    return pl.pallas_call(
        compact_kernel,
        out_shape=jax.ShapeDtypeStruct((RECV, COLS, C), B16),
        in_specs=[smem, vm],
        out_specs=anym,
        scratch_shapes=[pltpu.VMEM((COLS, C), B16), dma],
        compiler_params=pltpu.CompilerParams(vmem_limit_bytes=50 * 2**20),
    )(routes, pltpu.with_memory_space_constraint(recv, pltpu.VMEM))


def solution(mesh):
    in_specs = (P(("slide", "gy"), "gx", None),) + (P(),) * 9 + (P(("slide", "gy", "gx"), None),)
    out_specs = P(("slide", "gy", "gx"), None, None)
    return jax.shard_map(per_device, mesh=mesh, in_specs=in_specs, out_specs=out_specs, check_vma=False)
```

```python
import functools

import jax
import jax.numpy as jnp
import numpy as np
from jax import lax
from jax.experimental import pallas as pl
from jax.experimental.pallas import tpu as pltpu
from jax.sharding import PartitionSpec as P

B16 = jnp.bfloat16
F32 = jnp.float32
MESH = pl.DeviceIdType.MESH
GY, GX = 4, 8
N = GY * GX
SLOT = 3
RECV = 48
ROWS, COLS, C = 128, 128, 256
HID = 1024
EXT = COLS + 16
KS = 7


def shift_matrix():
    s = np.zeros((COLS, KS * EXT), np.float32)
    for b in range(KS):
        for j in range(COLS):
            s[j, b * EXT + (j + b - 3) % EXT] = 1.0
    return s


def pack_matrices():
    first = np.zeros((64, 256), np.float32)
    last = np.zeros((64, 256), np.float32)
    for u in range(16):
        for c in range(4):
            first[u * 4 + c, u * 16 + c] = 1.0
            last[u * 4 + c, u * 16 + 12 + c] = 1.0
    return first, last


def unpack_matrices():
    left = np.zeros((256, 64), np.float32)
    right = np.zeros((256, 64), np.float32)
    for u in range(16):
        for c in range(3):
            right[u * 16 + c, u * 4 + c] = 1.0
            left[u * 16 + 13 + c, u * 4 + 1 + c] = 1.0
    return left, right


def corner_matrix():
    m = np.zeros((96, 64), np.float32)
    for r in range(3):
        for c in range(3):
            m[r * 16 + 13 + c, (r + 1) * 4 + 1 + c] = 1.0
            m[r * 16 + c, 16 + (r + 1) * 4 + c] = 1.0
            m[48 + r * 16 + 13 + c, 32 + r * 4 + 1 + c] = 1.0
            m[48 + r * 16 + c, 48 + r * 4 + c] = 1.0
    return m


GROUPS = ((0, 1, 2), (3, 4), (5, 6))
CHIPS = (
    (2, 2), (1, 1), (3, 3), (2, 0), (0, 2), (1, 3), (3, 1), (2, 1),
    (1, 0), (2, 3), (3, 0), (1, 2), (0, 1), (3, 2), (0, 3),
)


def steps():
    every = [(z, x, t) for t in (1, 0) for z, x in CHIPS]
    far = sorted((o for o in every if 2 in o[:2]), key=lambda o: -(o[0] == 2) - (o[1] == 2))
    near = [o for o in every if 2 not in o[:2]]
    mixed = []
    for i in range(max(len(far), len(near))):
        mixed += far[i : i + 1] + near[i : i + 1]
    return mixed + [(0, 0, 1), (0, 0, 0)]


STEPS = steps()


def conv_group(xp, kb, rows, pp):
    for bs in GROUPS:
        w = {(a, b): kb[a * KS + b] for a in range(KS) for b in bs}

        def block(blk, _):
            o = pl.multiple_of(blk * 16, 16)
            for t, row in enumerate(rows):
                xs = [xp[row + a, pl.ds(o, 16), :] for a in range(KS)]
                for b in bs:
                    q = [xs[a] * w[(a, b)] for a in range(KS)]
                    s = ((q[0] + q[1]) + (q[2] + q[3])) + ((q[4] + q[5]) + q[6])
                    pp[t, pl.ds(b * EXT + o, 16), :] = s
            return 0

        lax.fori_loop(0, EXT // 16, block, 0)


def look_up(k, table):
    return sum(jnp.where(k == i, v, 0) for i, v in enumerate(table))


def block_kernel(
    route, x, sroute, kern, smat_h, pf, plast, ul, ur, cm, dbias, gain, nbias, uw_h, ub, dw_h, db, scale,
    recv, routes,
    xp, kb, pp, stage, hsend, hrecv, corner, smat, uw, dw,
    xsem, rows_s, rows_r, cols_s, cols_r, cor_s, cor_r, rt_s, rt_r, send_s, recv_s, own_s, w_s,
):
    sl = lax.axis_index("slide")
    gy = lax.axis_index("gy")
    gx = lax.axis_index("gx")
    me = gy * GX + gx

    def dev(y, z):
        return (sl, y, z)

    load = pltpu.make_async_copy(x, xp.at[pl.ds(3, ROWS), pl.ds(0, COLS)], xsem)
    load.start()

    barrier = pltpu.get_barrier_semaphore()

    def greet(k, _):
        r = (me + 1 + k) % N
        pl.semaphore_signal(barrier, inc=1, device_id=dev(r // GX, r % GX), device_id_type=MESH)
        return 0

    lax.fori_loop(0, N - 1, greet, 0)
    held = [
        pltpu.make_async_copy(h, v, w_s.at[i]) for i, (h, v) in enumerate(((smat_h, smat), (uw_h, uw), (dw_h, dw)))
    ]
    for h in held:
        h.start()

    for a in range(KS):
        for b in range(KS):
            kb[a * KS + b] = jnp.broadcast_to(kern[a, b : b + 1, :], (16, C)).astype(B16)

    up, down = (gy + GY - 1) % GY, (gy + 1) % GY
    left, right = (gx + GX - 1) % GX, (gx + 1) % GX

    def remote(src, dst, s, r, where):
        return pltpu.make_async_remote_copy(
            src_ref=src, dst_ref=dst, send_sem=s, recv_sem=r, device_id=where, device_id_type=MESH
        )

    halo_rows = [
        remote(x.at[pl.ds(0, 3)], xp.at[pl.ds(ROWS + 3, 3), pl.ds(0, COLS)], rows_s.at[0], rows_r.at[1], dev(up, gx)),
        remote(x.at[pl.ds(ROWS - 3, 3)], xp.at[pl.ds(0, 3), pl.ds(0, COLS)], rows_s.at[1], rows_r.at[0], dev(down, gx)),
    ]
    halo_cols = [
        remote(hsend.at[0], hrecv.at[1], cols_s.at[0], cols_r.at[1], dev(gy, left)),
        remote(hsend.at[1], hrecv.at[0], cols_s.at[1], cols_r.at[0], dev(gy, right)),
        remote(hsend.at[1, 7, pl.ds(48, 16)], corner.at[pl.ds(0, 16)], cor_s.at[0], cor_r.at[0], dev(down, right)),
        remote(hsend.at[0, 7, pl.ds(48, 16)], corner.at[pl.ds(16, 16)], cor_s.at[1], cor_r.at[1], dev(down, left)),
        remote(hsend.at[1, 0, pl.ds(0, 16)], corner.at[pl.ds(32, 16)], cor_s.at[2], cor_r.at[2], dev(up, right)),
        remote(hsend.at[0, 0, pl.ds(0, 16)], corner.at[pl.ds(48, 16)], cor_s.at[3], cor_r.at[3], dev(up, left)),
    ]

    pl.semaphore_wait(barrier, N - 1)
    for h in halo_rows:
        h.start()
    load.wait()
    for q in range(8):
        lo = xp[3 + q * 16 : 19 + q * 16, 0:16, :].reshape(256, C)
        hi = xp[3 + q * 16 : 19 + q * 16, COLS - 16 : COLS, :].reshape(256, C)
        hsend[0, q] = jnp.dot(pf[...], lo, preferred_element_type=F32).astype(B16)
        hsend[1, q] = jnp.dot(plast[...], hi, preferred_element_type=F32).astype(B16)
    for h in halo_cols:
        h.start()

    def place(k):
        core, cx = gx % 2, gx // 2
        a, b, t = (look_up(k, [o[i] for o in STEPS]) for i in range(3))
        dy, dx = jnp.where(core == 0, a, GY - b), jnp.where(core == 0, b, GX // 2 - a)
        return (gy + dy) % GY, ((cx + dx) % (GX // 2)) * 2 + (core + t) % 2

    def tell(k, _):
        ry, rx = place(k)
        remote(sroute, routes.at[me], rt_s, rt_r, dev(ry, rx)).start()
        return 0

    lax.fori_loop(0, N - 1, tell, 0)
    mine = pltpu.make_async_copy(sroute, routes.at[me], own_s.at[1])
    mine.start()

    for h in halo_cols:
        h.wait()

    @pl.when(gx == 0)
    def _():
        hrecv[0] = jnp.zeros_like(hrecv[0])
        corner[0:16] = jnp.zeros((16, C), B16)
        corner[32:48] = jnp.zeros((16, C), B16)

    @pl.when(gx == GX - 1)
    def _():
        hrecv[1] = jnp.zeros_like(hrecv[1])
        corner[16:32] = jnp.zeros((16, C), B16)
        corner[48:64] = jnp.zeros((16, C), B16)

    @pl.when(gy == 0)
    def _():
        corner[0:32] = jnp.zeros((32, C), B16)

    @pl.when(gy == GY - 1)
    def _():
        corner[32:64] = jnp.zeros((32, C), B16)

    for q in range(8):
        both = jnp.dot(ul[...], hrecv[0, q], preferred_element_type=F32) + jnp.dot(
            ur[...], hrecv[1, q], preferred_element_type=F32
        )
        xp[3 + q * 16 : 19 + q * 16, COLS:EXT, :] = both.astype(B16).reshape(16, 16, C)
    edge = jnp.dot(cm[...], corner[...], preferred_element_type=F32).astype(B16).reshape(2, 3, 16, C)
    xp[0:3, COLS:EXT, :] = edge[0]
    xp[ROWS + 3 : ROWS + 6, COLS:EXT, :] = edge[1]

    for h in halo_rows:
        h.wait()

    @pl.when(gy == 0)
    def _():
        xp[0:3, 0:COLS] = jnp.zeros((3, COLS, C), B16)

    @pl.when(gy == GY - 1)
    def _():
        xp[ROWS + 3 : ROWS + 6, 0:COLS] = jnp.zeros((3, COLS, C), B16)

    for h in held:
        h.wait()

    def compute(k):
        ry, rx = place(k)
        r = ry * GX + rx
        rows = [jnp.maximum(route[0, r * SLOT + t], 0) for t in range(SLOT)]
        normed = []
        conv_group(xp, kb, rows, pp)
        for t in range(SLOT):
            d = jnp.dot(smat[...], pp[t], preferred_element_type=F32) + dbias[...]
            c = d - jnp.mean(d, axis=1, keepdims=True)
            v = jnp.mean(c * c, axis=1, keepdims=True)
            normed.append((c * lax.rsqrt(v + 1e-6) * gain[...] + nbias[...]).astype(B16))
        n = jnp.concatenate(normed, axis=0)
        branch = None
        for q in range(4):
            qs = slice(q * 256, (q + 1) * 256)
            hh = jnp.dot(n, uw[:, qs], preferred_element_type=F32) + ub[:, qs]
            g = (0.5 * hh * (1.0 + lax.erf(hh * 0.7071067811865476))).astype(B16)
            part = jnp.dot(g, dw[qs, :], preferred_element_type=F32)
            branch = part if branch is None else branch + part
        branch = branch + db[...]
        for t in range(SLOT):
            o = xp[rows[t] + 3, 0:COLS, :].astype(F32) + scale[...] * branch[t * COLS : (t + 1) * COLS]
            stage[k, t] = o.astype(B16)
        return ry, rx

    def step(k, _):
        ry, rx = compute(k)

        @pl.when(k < N - 1)
        def _():
            remote(stage.at[k], recv.at[me], send_s, recv_s, dev(ry, rx)).start()

        @pl.when(k == N - 1)
        def _():
            pltpu.make_async_copy(stage.at[k], recv.at[me], own_s.at[0]).start()

        return 0

    lax.fori_loop(0, N, step, 0)
    mine.wait()
    pltpu.make_async_copy(stage.at[N - 1], recv.at[me], own_s.at[0]).wait()
    several = routes.at[pl.ds(0, N - 1)]
    pltpu.make_async_copy(several, several, rt_s).wait()
    pltpu.make_async_copy(several, several, rt_r).wait()

    sent = stage.at[pl.ds(0, N - 1)]
    pltpu.make_async_copy(sent, sent, send_s).wait()
    pltpu.make_async_copy(sent, sent, recv_s).wait()


def compact_kernel(routes, recv, out, zero, sem):
    me = lax.axis_index("gy") * GX + lax.axis_index("gx")
    zero[...] = jnp.zeros_like(zero)

    def look(i, count):
        g, s = i // SLOT, i % SLOT
        take = jnp.logical_and(routes[g, 0, me * SLOT + s] >= 0, count < RECV)

        @pl.when(take)
        def _():
            pltpu.make_async_copy(recv.at[g, s], out.at[count], sem).start()

        return count + take.astype(jnp.int32)

    count = lax.fori_loop(0, N * SLOT, look, jnp.int32(0))

    def blank(k, _):
        pltpu.make_async_copy(zero, out.at[k], sem).start()
        return 0

    lax.fori_loop(count, RECV, blank, 0)
    pltpu.make_async_copy(out, out, sem).wait()


def per_device(
    feature_map, depth_kernel, depth_bias, norm_gain, norm_bias, up_weight, up_bias, down_weight, down_bias,
    layer_scale, tile_route,
):
    vm = pl.BlockSpec(memory_space=pltpu.VMEM)
    anym = pl.BlockSpec(memory_space=pl.ANY)
    smem = pl.BlockSpec(memory_space=pltpu.SMEM)
    pf, plast = pack_matrices()
    ul, ur = unpack_matrices()
    const = [jnp.asarray(m, B16) for m in (shift_matrix(), pf, plast, ul, ur, corner_matrix())]
    row = lambda a: a.reshape(1, -1)
    dma = pltpu.SemaphoreType.DMA
    recv, routes = pl.pallas_call(
        block_kernel,
        out_shape=(
            pltpu.VMEM((N, SLOT, COLS, C), B16),
            jax.ShapeDtypeStruct((N, 1, N * SLOT), jnp.int32),
        ),
        in_specs=[smem, anym, anym, vm, anym] + [vm] * 8 + [anym, vm, anym, vm, vm],
        out_specs=(vm, anym),
        scratch_shapes=[
            pltpu.VMEM((ROWS + 6, EXT, C), B16),
            pltpu.VMEM((KS * KS, 16, C), B16),
            pltpu.VMEM((SLOT, KS * EXT, C), B16),
            pltpu.VMEM((N, SLOT, COLS, C), B16),
            pltpu.VMEM((2, 8, 64, C), B16),
            pltpu.VMEM((2, 8, 64, C), B16),
            pltpu.VMEM((64, C), B16),
            pltpu.VMEM((COLS, KS * EXT), B16),
            pltpu.VMEM((C, HID), B16),
            pltpu.VMEM((HID, C), B16),
            dma,
            dma((2,)), dma((2,)), dma((2,)), dma((2,)), dma((4,)), dma((4,)),
            dma, dma, dma, dma, dma((2,)), dma((3,)),
        ],
        compiler_params=pltpu.CompilerParams(
            collective_id=0, has_side_effects=True, vmem_limit_bytes=50 * 2**20
        ),
    )(
        tile_route, feature_map, tile_route, depth_kernel, *const, row(depth_bias),
        row(norm_gain), row(norm_bias), up_weight, row(up_bias), down_weight, row(down_bias), row(layer_scale),
    )
    return pl.pallas_call(
        compact_kernel,
        out_shape=jax.ShapeDtypeStruct((RECV, COLS, C), B16),
        in_specs=[smem, vm],
        out_specs=anym,
        scratch_shapes=[pltpu.VMEM((COLS, C), B16), dma],
        compiler_params=pltpu.CompilerParams(vmem_limit_bytes=50 * 2**20),
    )(routes, pltpu.with_memory_space_constraint(recv, pltpu.VMEM))


def solution(mesh):
    in_specs = (P(("slide", "gy"), "gx", None),) + (P(),) * 9 + (P(("slide", "gy", "gx"), None),)
    out_specs = P(("slide", "gy", "gx"), None, None)
    return jax.shard_map(per_device, mesh=mesh, in_specs=in_specs, out_specs=out_specs, check_vma=False)
```

```python
import functools

import jax
import jax.numpy as jnp
import numpy as np
from jax import lax
from jax.experimental import pallas as pl
from jax.experimental.pallas import tpu as pltpu
from jax.sharding import PartitionSpec as P

B16 = jnp.bfloat16
F32 = jnp.float32
MESH = pl.DeviceIdType.MESH
GY, GX = 4, 8
N = GY * GX
SLOT = 3
RECV = 48
ROWS, COLS, C = 128, 128, 256
HID = 1024
EXT = COLS + 16
KS = 7
HALF = 256


def shift_matrix():
    s = np.zeros((COLS, KS * EXT), np.float32)
    for b in range(KS):
        for j in range(COLS):
            s[j, b * EXT + (j + b - 3) % EXT] = 1.0
    return s


def pack_matrices():
    first = np.zeros((64, 256), np.float32)
    last = np.zeros((64, 256), np.float32)
    for u in range(16):
        for c in range(4):
            first[u * 4 + c, u * 16 + c] = 1.0
            last[u * 4 + c, u * 16 + 12 + c] = 1.0
    return first, last


def unpack_matrices():
    left = np.zeros((256, 64), np.float32)
    right = np.zeros((256, 64), np.float32)
    for u in range(16):
        for c in range(3):
            right[u * 16 + c, u * 4 + c] = 1.0
            left[u * 16 + 13 + c, u * 4 + 1 + c] = 1.0
    return left, right


def corner_matrix():
    m = np.zeros((96, 64), np.float32)
    for r in range(3):
        for c in range(3):
            m[r * 16 + 13 + c, (r + 1) * 4 + 1 + c] = 1.0
            m[r * 16 + c, 16 + (r + 1) * 4 + c] = 1.0
            m[48 + r * 16 + 13 + c, 32 + r * 4 + 1 + c] = 1.0
            m[48 + r * 16 + c, 48 + r * 4 + c] = 1.0
    return m


GROUPS = ((0, 1, 2), (3, 4), (5, 6))
CHIPS = (
    (2, 2), (1, 1), (3, 3), (2, 0), (0, 2), (1, 3), (3, 1), (2, 1),
    (1, 0), (2, 3), (3, 0), (1, 2), (0, 1), (3, 2), (0, 3),
)


def steps():
    every = [(z, x, t) for t in (1, 0) for z, x in CHIPS]
    far = sorted((o for o in every if 2 in o[:2]), key=lambda o: -(o[0] == 2) - (o[1] == 2))
    near = [o for o in every if 2 not in o[:2]]
    mixed = []
    for i in range(max(len(far), len(near))):
        mixed += far[i : i + 1] + near[i : i + 1]
    return mixed + [(0, 0, 1), (0, 0, 0)]


STEPS = steps()


def conv_group(xp, kb, rows, pp):
    for bs in GROUPS:
        w = {(a, b): kb[a * KS + b] for a in range(KS) for b in bs}

        def block(blk, _):
            o = pl.multiple_of(blk * 16, 16)
            for t, row in enumerate(rows):
                xs = [xp[row + a, pl.ds(o, 16), :] for a in range(KS)]
                for b in bs:
                    q = [xs[a] * w[(a, b)] for a in range(KS)]
                    s = ((q[0] + q[1]) + (q[2] + q[3])) + ((q[4] + q[5]) + q[6])
                    pp[t, pl.ds(b * EXT + o, 16), :] = s
            return 0

        lax.fori_loop(0, EXT // 16, block, 0)


def look_up(k, table):
    return sum(jnp.where(k == i, v, 0) for i, v in enumerate(table))


def block_kernel(
    route, x, sroute, kern, smat_h, pf, plast, ul, ur, cm, dbias, gain, nbias, uw_h, ub, dw_h, db, scale,
    recv, routes,
    xp, kb, pp, stage, hsend, hrecv, corner, smat, uw, dw,
    xsem, rows_s, rows_r, cols_s, cols_r, cor_s, cor_r, rt_s, rt_r, send_s, recv_s, own_s, w_s,
):
    sl = lax.axis_index("slide")
    gy = lax.axis_index("gy")
    gx = lax.axis_index("gx")
    me = gy * GX + gx

    def dev(y, z):
        return (sl, y, z)

    load = pltpu.make_async_copy(x, xp.at[pl.ds(3, ROWS), pl.ds(0, COLS)], xsem)
    load.start()

    barrier = pltpu.get_barrier_semaphore()

    def greet(k, _):
        r = (me + 1 + k) % N
        pl.semaphore_signal(barrier, inc=1, device_id=dev(r // GX, r % GX), device_id_type=MESH)
        return 0

    lax.fori_loop(0, N - 1, greet, 0)
    held = [
        pltpu.make_async_copy(h, v, w_s.at[i]) for i, (h, v) in enumerate(((smat_h, smat), (uw_h, uw), (dw_h, dw)))
    ]
    for h in held:
        h.start()

    for a in range(KS):
        for b in range(KS):
            kb[a * KS + b] = jnp.broadcast_to(kern[a, b : b + 1, :], (16, C)).astype(B16)

    up, down = (gy + GY - 1) % GY, (gy + 1) % GY
    left, right = (gx + GX - 1) % GX, (gx + 1) % GX

    def remote(src, dst, s, r, where):
        return pltpu.make_async_remote_copy(
            src_ref=src, dst_ref=dst, send_sem=s, recv_sem=r, device_id=where, device_id_type=MESH
        )

    halo_rows = [
        remote(x.at[pl.ds(0, 3)], xp.at[pl.ds(ROWS + 3, 3), pl.ds(0, COLS)], rows_s.at[0], rows_r.at[1], dev(up, gx)),
        remote(x.at[pl.ds(ROWS - 3, 3)], xp.at[pl.ds(0, 3), pl.ds(0, COLS)], rows_s.at[1], rows_r.at[0], dev(down, gx)),
    ]
    halo_cols = [
        remote(hsend.at[0], hrecv.at[1], cols_s.at[0], cols_r.at[1], dev(gy, left)),
        remote(hsend.at[1], hrecv.at[0], cols_s.at[1], cols_r.at[0], dev(gy, right)),
        remote(hsend.at[1, 7, pl.ds(48, 16)], corner.at[pl.ds(0, 16)], cor_s.at[0], cor_r.at[0], dev(down, right)),
        remote(hsend.at[0, 7, pl.ds(48, 16)], corner.at[pl.ds(16, 16)], cor_s.at[1], cor_r.at[1], dev(down, left)),
        remote(hsend.at[1, 0, pl.ds(0, 16)], corner.at[pl.ds(32, 16)], cor_s.at[2], cor_r.at[2], dev(up, right)),
        remote(hsend.at[0, 0, pl.ds(0, 16)], corner.at[pl.ds(48, 16)], cor_s.at[3], cor_r.at[3], dev(up, left)),
    ]

    pl.semaphore_wait(barrier, N - 1)
    for h in halo_rows:
        h.start()
    load.wait()
    for q in range(8):
        lo = xp[3 + q * 16 : 19 + q * 16, 0:16, :].reshape(256, C)
        hi = xp[3 + q * 16 : 19 + q * 16, COLS - 16 : COLS, :].reshape(256, C)
        hsend[0, q] = jnp.dot(pf[...], lo, preferred_element_type=F32).astype(B16)
        hsend[1, q] = jnp.dot(plast[...], hi, preferred_element_type=F32).astype(B16)
    for h in halo_cols:
        h.start()

    def place(k):
        core, cx = gx % 2, gx // 2
        a, b, t = (look_up(k, [o[i] for o in STEPS]) for i in range(3))
        dy, dx = jnp.where(core == 0, a, GY - b), jnp.where(core == 0, b, GX // 2 - a)
        return (gy + dy) % GY, ((cx + dx) % (GX // 2)) * 2 + (core + t) % 2

    def tell(k, _):
        ry, rx = place(k)
        remote(sroute, routes.at[me], rt_s, rt_r, dev(ry, rx)).start()
        return 0

    lax.fori_loop(0, N - 1, tell, 0)
    mine = pltpu.make_async_copy(sroute, routes.at[me], own_s.at[1])
    mine.start()

    for h in halo_cols:
        h.wait()

    @pl.when(gx == 0)
    def _():
        hrecv[0] = jnp.zeros_like(hrecv[0])
        corner[0:16] = jnp.zeros((16, C), B16)
        corner[32:48] = jnp.zeros((16, C), B16)

    @pl.when(gx == GX - 1)
    def _():
        hrecv[1] = jnp.zeros_like(hrecv[1])
        corner[16:32] = jnp.zeros((16, C), B16)
        corner[48:64] = jnp.zeros((16, C), B16)

    @pl.when(gy == 0)
    def _():
        corner[0:32] = jnp.zeros((32, C), B16)

    @pl.when(gy == GY - 1)
    def _():
        corner[32:64] = jnp.zeros((32, C), B16)

    for q in range(8):
        both = jnp.dot(ul[...], hrecv[0, q], preferred_element_type=F32) + jnp.dot(
            ur[...], hrecv[1, q], preferred_element_type=F32
        )
        xp[3 + q * 16 : 19 + q * 16, COLS:EXT, :] = both.astype(B16).reshape(16, 16, C)
    edge = jnp.dot(cm[...], corner[...], preferred_element_type=F32).astype(B16).reshape(2, 3, 16, C)
    xp[0:3, COLS:EXT, :] = edge[0]
    xp[ROWS + 3 : ROWS + 6, COLS:EXT, :] = edge[1]

    for h in halo_rows:
        h.wait()

    @pl.when(gy == 0)
    def _():
        xp[0:3, 0:COLS] = jnp.zeros((3, COLS, C), B16)

    @pl.when(gy == GY - 1)
    def _():
        xp[ROWS + 3 : ROWS + 6, 0:COLS] = jnp.zeros((3, COLS, C), B16)

    for h in held:
        h.wait()

    def compute(k, groups):
        where = [place(k + i) for i in range(groups)]
        count = groups * SLOT
        rows = [
            jnp.maximum(route[0, (ry * GX + rx) * SLOT + t], 0) for ry, rx in where for t in range(SLOT)
        ]
        conv_group(xp, kb, rows, pp)
        normed = []
        for t in range(count):
            d = jnp.dot(smat[...], pp[t], preferred_element_type=F32) + dbias[...]
            c = d - jnp.mean(d, axis=1, keepdims=True)
            v = jnp.mean(c * c, axis=1, keepdims=True)
            normed.append((c * lax.rsqrt(v + 1e-6) * gain[...] + nbias[...]).astype(B16))
        n = jnp.concatenate(normed, axis=0)
        branch = None
        for q in range(HID // HALF):
            qs = slice(q * HALF, (q + 1) * HALF)
            hh = jnp.dot(n, uw[:, qs], preferred_element_type=F32) + ub[:, qs]
            g = (0.5 * hh * (1.0 + lax.erf(hh * 0.7071067811865476))).astype(B16)
            part = jnp.dot(g, dw[qs, :], preferred_element_type=F32)
            branch = part if branch is None else branch + part
        branch = branch + db[...]
        for t in range(count):
            o = xp[rows[t] + 3, 0:COLS, :].astype(F32) + scale[...] * branch[t * COLS : (t + 1) * COLS]
            stage[k + t // SLOT, t % SLOT] = o.astype(B16)
        return where

    def send(k, ry, rx):
        remote(stage.at[k], recv.at[me], send_s, recv_s, dev(ry, rx)).start()

    def single(k, _):
        ((ry, rx),) = compute(k, 1)
        send(k, ry, rx)
        return 0

    def double(j, _):
        k = 2 * j
        (ry, rx), (sy, sx) = compute(k, 2)
        send(k, ry, rx)

        @pl.when(k + 1 < N - 1)
        def _():
            send(k + 1, sy, sx)

        @pl.when(k + 1 == N - 1)
        def _():
            pltpu.make_async_copy(stage.at[k + 1], recv.at[me], own_s.at[0]).start()

        return 0

    lax.fori_loop(0, 2, single, 0)
    lax.fori_loop(1, N // 2, double, 0)
    mine.wait()
    pltpu.make_async_copy(stage.at[N - 1], recv.at[me], own_s.at[0]).wait()
    several = routes.at[pl.ds(0, N - 1)]
    pltpu.make_async_copy(several, several, rt_s).wait()
    pltpu.make_async_copy(several, several, rt_r).wait()

    sent = stage.at[pl.ds(0, N - 1)]
    pltpu.make_async_copy(sent, sent, send_s).wait()
    pltpu.make_async_copy(sent, sent, recv_s).wait()


def compact_kernel(routes, recv, out, zero, sem):
    me = lax.axis_index("gy") * GX + lax.axis_index("gx")
    zero[...] = jnp.zeros_like(zero)

    def look(i, count):
        g, s = i // SLOT, i % SLOT
        take = jnp.logical_and(routes[g, 0, me * SLOT + s] >= 0, count < RECV)

        @pl.when(take)
        def _():
            pltpu.make_async_copy(recv.at[g, s], out.at[count], sem).start()

        return count + take.astype(jnp.int32)

    count = lax.fori_loop(0, N * SLOT, look, jnp.int32(0))

    def blank(k, _):
        pltpu.make_async_copy(zero, out.at[k], sem).start()
        return 0

    lax.fori_loop(count, RECV, blank, 0)
    pltpu.make_async_copy(out, out, sem).wait()


def per_device(
    feature_map, depth_kernel, depth_bias, norm_gain, norm_bias, up_weight, up_bias, down_weight, down_bias,
    layer_scale, tile_route,
):
    vm = pl.BlockSpec(memory_space=pltpu.VMEM)
    anym = pl.BlockSpec(memory_space=pl.ANY)
    smem = pl.BlockSpec(memory_space=pltpu.SMEM)
    pf, plast = pack_matrices()
    ul, ur = unpack_matrices()
    const = [jnp.asarray(m, B16) for m in (shift_matrix(), pf, plast, ul, ur, corner_matrix())]
    row = lambda a: a.reshape(1, -1)
    dma = pltpu.SemaphoreType.DMA
    recv, routes = pl.pallas_call(
        block_kernel,
        out_shape=(
            pltpu.VMEM((N, SLOT, COLS, C), B16),
            jax.ShapeDtypeStruct((N, 1, N * SLOT), jnp.int32),
        ),
        in_specs=[smem, anym, anym, vm, anym] + [vm] * 8 + [anym, vm, anym, vm, vm],
        out_specs=(vm, anym),
        scratch_shapes=[
            pltpu.VMEM((ROWS + 6, EXT, C), B16),
            pltpu.VMEM((KS * KS, 16, C), B16),
            pltpu.VMEM((2 * SLOT, KS * EXT, C), B16),
            pltpu.VMEM((N, SLOT, COLS, C), B16),
            pltpu.VMEM((2, 8, 64, C), B16),
            pltpu.VMEM((2, 8, 64, C), B16),
            pltpu.VMEM((64, C), B16),
            pltpu.VMEM((COLS, KS * EXT), B16),
            pltpu.VMEM((C, HID), B16),
            pltpu.VMEM((HID, C), B16),
            dma,
            dma((2,)), dma((2,)), dma((2,)), dma((2,)), dma((4,)), dma((4,)),
            dma, dma, dma, dma, dma((2,)), dma((3,)),
        ],
        compiler_params=pltpu.CompilerParams(
            collective_id=0, has_side_effects=True, vmem_limit_bytes=50 * 2**20
        ),
    )(
        tile_route, feature_map, tile_route, depth_kernel, *const, row(depth_bias),
        row(norm_gain), row(norm_bias), up_weight, row(up_bias), down_weight, row(down_bias), row(layer_scale),
    )
    return pl.pallas_call(
        compact_kernel,
        out_shape=jax.ShapeDtypeStruct((RECV, COLS, C), B16),
        in_specs=[smem, vm],
        out_specs=anym,
        scratch_shapes=[pltpu.VMEM((COLS, C), B16), dma],
        compiler_params=pltpu.CompilerParams(vmem_limit_bytes=50 * 2**20),
    )(routes, pltpu.with_memory_space_constraint(recv, pltpu.VMEM))


def solution(mesh):
    in_specs = (P(("slide", "gy"), "gx", None),) + (P(),) * 9 + (P(("slide", "gy", "gx"), None),)
    out_specs = P(("slide", "gy", "gx"), None, None)
    return jax.shard_map(per_device, mesh=mesh, in_specs=in_specs, out_specs=out_specs, check_vma=False)
```
